32 devices in a mesh: feeder: 2 (over y), tm: 16 (over z, x, core).
Axes of the slice: x: 2, y: 2, z: 4, core: 2. Of those that a mesh axis runs over, the one named last changes fastest.
Arguments:
- observed: bfloat16 [6144, 8192], P('feeder', 'tm'), may hold values from -6 to 6
- mask_words: int32 [6144, 1024], P('feeder', 'tm'), may hold values from 0 to 255, as said below
- feeder_factor: float32 [6144, 64], P('feeder'), may hold values from -6 to 6
- time_factor: float32 [64, 8192], P(None, 'tm'), may hold values from -0.75 to 0.75
- ar_weight: float32 [10, 64], replicated, may hold values from -0.5 to 0.5
- lags: int32 [10], replicated, may hold values from 1 to 1440, as said below
- moment_first: float32 [6144, 64], P(('feeder', 'tm')), may hold values from -0.6 to 0.6
- moment_second: float32 [6144, 64], P(('feeder', 'tm')), may hold values from 0.01 to 1
Outputs:
- new_factor: float32 [6144, 64], P(('feeder', 'tm'))
- new_first: float32 [6144, 64], P(('feeder', 'tm'))
- new_second: float32 [6144, 64], P(('feeder', 'tm'))
- time_grad: float32 [64, 8192], P('feeder', 'tm')
The draws below stay inside these ranges and needn't reach their ends.
Inputs may be any that keep to these rules, and one draw needn't show every extreme that they name: `mask_words`: bit b of word w of a feeder's row tells whether minute 8 w + b is observed (1) or not (0). Eight lags of 1 to 12, one lag between 30 and 90, and one lag of exactly 1440; lags may repeat.
All inputs are finite; a program needn't handle non-finite values.
Results may differ from the reference program's by a relative error of at most 0.00065.
Values sent between devices are 32-bit elements; how exact they have to be, the bound alone decides.
A program may use at most 64 MiB of HBM per device.

```python
import math
import jax
import jax.numpy as jnp
from jax import lax

K = 64
NLAG = 10
LAGMAX = 1440
NF = 3072
N = 6144
T_SIZE = 8192
WORDS = 1024
N_FEEDER = 2


def draw_mask_words(key, part):
    base_key = jax.random.fold_in(key, 5)
    place_key = jax.random.fold_in(key, 7)
    words = jax.random.randint(base_key, (N, WORDS), 0, 256, dtype=jnp.int32)
    row_pick = jax.random.randint(place_key, (), 0, N, dtype=jnp.int32)
    word_pick = jax.random.randint(jax.random.fold_in(place_key, 1), (), 0, WORDS, dtype=jnp.int32)
    words = words.at[row_pick, word_pick].set(jnp.int32(0))
    words = words.at[(row_pick + 1) % N, word_pick].set(jnp.int32(255))
    return words


def draw_lags(key, part):
    first_key = jax.random.fold_in(key, 11)
    second_key = jax.random.fold_in(key, 23)
    short_lags = jax.random.permutation(first_key, 12)[:8].astype(jnp.int32) + 1
    middle = jax.random.randint(second_key, (1,), max(LAGMAX // 48, 1), LAGMAX // 16 + 1, dtype=jnp.int32)
    longest = jnp.full((1,), LAGMAX, dtype=jnp.int32)
    return jnp.concatenate([short_lags, middle, longest]).astype(jnp.int32)


def with_spikes(array, rng, source, target, parts, factor):
    owner, partner = [(jnp.arange(array.shape[axis_at]) // (array.shape[axis_at] // parts)).reshape([-1 if axis == axis_at else 1 for axis in range(array.ndim)]) for axis_at in (source, target)]
    chosen = jax.random.permutation(rng, parts)[partner]
    strong = (owner == chosen) | (owner == (partner + parts // 2) % parts)
    return jnp.where(strong, factor * array, array)


def shard_levels(rng, shape, split, smallest, high):
    loudness = 1.0
    for dim, parts in split:
        steps = jax.random.uniform(jax.random.fold_in(jax.random.fold_in(rng, 6), dim), (parts,), jnp.float32, smallest / len(split), high / len(split))
        loudness = loudness * jnp.repeat(jnp.exp(steps), shape[dim] // parts).reshape((-1,) + (1,) * (len(shape) - 1 - dim))
    return loudness


def noise(key, dims, spread, most, shards=(), held_as=jnp.bfloat16):
    gain = shard_levels(key, dims, shards, -0.22, 0.18) if shards else 1.0
    array = jax.random.normal(key, dims, jnp.float32) * spread * gain
    return jnp.minimum(jnp.maximum(array, -most), most).astype(held_as)


def noise_with(own_key, shape, scale, reach, shards, heavy, held_as=jnp.bfloat16):
    drawn = scale * jax.random.normal(own_key, shape, jnp.float32)
    if shards:
        drawn = drawn * shard_levels(own_key, shape, shards, -0.22, 0.18)
    return jnp.clip(with_spikes(drawn, jax.random.fold_in(own_key, 3), *heavy), -reach, reach).astype(held_as)


def setup_inputs(seed: int = 0) -> dict:
    key_of = jax.random.split(jax.random.key(seed), 9)
    observed = noise_with(key_of[0], (N, T_SIZE), 1.0, 6.0, ((0, 2), (1, 16)), (1, 0, 16, 2.0))
    mask_words = draw_mask_words(jax.random.fold_in(key_of[8], 71), 0)
    feeder_factor = noise(key_of[2], (N, K), 1.0, 6.0, ((0, 2),), jnp.float32)
    time_factor = noise(key_of[3], (K, T_SIZE), 0.125, 0.75, ((1, 16),), jnp.float32)
    ar_weight = jnp.clip(jax.random.uniform(key_of[4], (NLAG, K), jnp.float32, -0.5, 0.5), -0.5, 0.5)
    lags = draw_lags(jax.random.fold_in(key_of[8], 71), 0)
    moment_first = noise(key_of[6], (N, K), 0.1, 0.6, ((0, 32),), jnp.float32)
    moment_second = jnp.clip(jnp.exp(math.log(1.0) - 4.6051702 * jax.random.uniform(key_of[7], (N, K), jnp.float32) ** shard_levels(key_of[7], (N, K), ((0, 32),), -0.2, 0.2)), 0.01, 1.0)
    return {"observed": observed, "mask_words": mask_words, "feeder_factor": feeder_factor, "time_factor": time_factor, "ar_weight": ar_weight, "lags": lags, "moment_first": moment_first, "moment_second": moment_second}


DATA_WEIGHT = 1.0 / 64.0
LAM_F = 0.1
LAM_X = 0.01
LAM_AR = 8.0
BETA_ONE = 0.9
BETA_TWO = 0.999
BIAS_FIRST = 1.0 - 0.9 ** 8
BIAS_SECOND = 1.0 - 0.999 ** 8
LEARNING_RATE = 0.05
ADAM_EPS = 1e-08

def unpack_mask(words):
    shifts = jnp.arange(8, dtype=jnp.int32)
    bits = words[:, :, None] >> shifts & 1
    return bits.reshape(words.shape[0], words.shape[1] * 8).astype(jnp.float32)

def reference(observed, mask_words, feeder_factor, time_factor, ar_weight, lags, moment_first, moment_second):
    time_half = time_factor.astype(jnp.bfloat16)
    obs_blocks = observed.reshape(N_FEEDER, NF, T_SIZE)
    word_blocks = mask_words.reshape(N_FEEDER, NF, WORDS)
    factor_blocks = feeder_factor.reshape(N_FEEDER, NF, K)

    def block_terms(carry, pieces):
        obs_block, word_block, factor_block = pieces
        factor_half = factor_block.astype(jnp.bfloat16)
        predicted = jnp.dot(factor_half, time_half, preferred_element_type=jnp.float32)
        residual = (unpack_mask(word_block) * (predicted - obs_block.astype(jnp.float32))).astype(jnp.bfloat16)
        grad_rows = jnp.dot(residual, time_half.T, preferred_element_type=jnp.float32)
        time_term = lax.dot_general(factor_half, residual, (((0,), (0,)), ((), ())), preferred_element_type=jnp.float32)
        return (carry + time_term, grad_rows)
    time_data, grad_blocks = lax.scan(block_terms, jnp.zeros((K, T_SIZE), jnp.float32), (obs_blocks, word_blocks, factor_blocks))
    factor_grad = DATA_WEIGHT * grad_blocks.reshape(N, K) + LAM_F * feeder_factor
    padded = jnp.concatenate([jnp.zeros((K, LAGMAX), jnp.float32), time_factor], axis=1)
    predicted_ar = jnp.zeros((K, T_SIZE), jnp.float32)
    for index in range(NLAG):
        start = (LAGMAX - lags[index]).astype(jnp.int32)
        predicted_ar = predicted_ar + ar_weight[index][:, None] * lax.dynamic_slice_in_dim(padded, start, T_SIZE, 1)
    columns = jnp.arange(T_SIZE, dtype=jnp.int32)
    errors = jnp.where(columns[None, :] >= LAGMAX, time_factor - predicted_ar, 0.0)
    ahead = jnp.concatenate([errors, jnp.zeros((K, LAGMAX), jnp.float32)], axis=1)
    carried = jnp.zeros((K, T_SIZE), jnp.float32)
    for index in range(NLAG):
        start = lags[index].astype(jnp.int32)
        carried = carried + ar_weight[index][:, None] * lax.dynamic_slice_in_dim(ahead, start, T_SIZE, 1)
    adjoint = errors - carried
    time_grad = DATA_WEIGHT * time_data + LAM_AR * adjoint + LAM_X * time_factor
    new_first = BETA_ONE * moment_first + (1.0 - BETA_ONE) * factor_grad
    new_second = BETA_TWO * moment_second + (1.0 - BETA_TWO) * factor_grad * factor_grad
    update = LEARNING_RATE * (new_first / BIAS_FIRST) / (jnp.sqrt(new_second / BIAS_SECOND) + ADAM_EPS)
    new_factor = feeder_factor - update
    return (new_factor, new_first, new_second, time_grad)
```

```python
import functools

import jax
import jax.numpy as jnp
from jax import lax
from jax.experimental import pallas as pl
from jax.experimental.pallas import tpu as pltpu
from jax.sharding import PartitionSpec as P

LAGMAX = 1440
LANES = 128
MESH = pl.DeviceIdType.MESH

DATA_WEIGHT = 1.0 / 64.0
LAM_F = 0.1
LAM_X = 0.01
LAM_AR = 8.0
BETA_ONE = 0.9
BETA_TWO = 0.999
BIAS_FIRST = 1.0 - 0.9**8
BIAS_SECOND = 1.0 - 0.999**8
LEARNING_RATE = 0.05
ADAM_EPS = 1e-08


def xor(a, b, count):
    total = 0
    bit = 1
    while bit < count:
        total = total + bit * ((a // bit + b // bit) % 2)
        bit *= 2
    return total


def halo_pieces(span):
    blocks = span // LANES
    far = -(-LAGMAX // LANES)
    wanted = (
        list(range(-far, blocks + 2 - far))
        + list(range(-1, blocks + 1))
        + list(range(far - 2, far + blocks))
    )
    pieces = []
    for slot, block in enumerate(wanted):
        distance, place = divmod(block, blocks)
        if distance == 0:
            continue
        last = pieces[-1] if pieces else None
        if last and last[0] == distance and last[1] + last[3] == place and last[2] + last[3] == slot:
            last[3] += 1
        else:
            pieces.append([distance, place, slot, 1])
    return pieces, len(wanted)


def kernel(
    feeders, tms, chunk, share,
    obs_hbm, words_hbm, factor_hbm, time_ref, weight_ref, lags_ref, first_ref, second_ref,
    new_factor_ref, new_first_ref, new_second_ref, time_grad_ref,
    obs, words, factor, rhs_wide, rhs_back, window, weights,
    parts, pair, sums, landed, time_part, time_landed,
    in_sem, pair_send, pair_recv, sum_send, sum_recv, time_send, time_recv, halo_send, halo_recv,
):
    ranks, span = time_ref.shape
    rows = obs_hbm.shape[0]
    steps = rows // chunk
    members = chunk // share
    pairs = members // 2
    half = share // 2
    band = ranks // feeders
    f = lax.axis_index("feeder")
    tm = lax.axis_index("tm")
    core = tm % 2
    my_chunk = tm // members
    my_pair = (tm // 2) % pairs
    partner = tm + 1 - 2 * core
    band_rows = pl.ds(pl.multiple_of(f * band, 8), band)
    pieces, slots = halo_pieces(span)
    blocks = span // LANES

    def loads(s):
        start = pl.multiple_of(xor(my_chunk, steps - 1 - s, steps) * chunk, LANES)
        where = pl.ds(start, chunk)
        return (
            pltpu.make_async_copy(obs_hbm.at[where, :], obs.at[s], in_sem.at[0, s]),
            pltpu.make_async_copy(words_hbm.at[:, where], words.at[s], in_sem.at[1, s]),
            pltpu.make_async_copy(factor_hbm.at[:, where], factor.at[s], in_sem.at[2, s]),
        )

    for s in range(steps):
        for copy in loads(s):
            copy.start()

    window[...] = jnp.zeros_like(window)
    barrier = pltpu.get_barrier_semaphore()

    @pl.loop(1, tms)
    def _(k):
        pl.semaphore_signal(barrier, inc=1, device_id=(f, (tm + k) % tms), device_id_type=MESH)

    for k in range(1, feeders):
        pl.semaphore_signal(barrier, inc=1, device_id=((f + k) % feeders, tm), device_id_type=MESH)

    time_all = time_ref[...]
    time_zero = jnp.zeros_like(time_all)
    wide = span // 8
    column = lax.broadcasted_iota(jnp.int32, (wide, span), 1)
    word = lax.broadcasted_iota(jnp.int32, (wide, span), 0)
    level = jnp.left_shift(jnp.int32(1), 7 - jnp.bitwise_and(column, 7)).astype(jnp.float32) * (1.0 / 128.0)
    spread = jnp.where(jnp.right_shift(column, 3) == word, level, 0.0)
    rhs_wide[0:ranks, 0:span] = time_all.astype(jnp.bfloat16)
    rhs_wide[0:ranks, span : 2 * span] = jnp.zeros((ranks, span), jnp.bfloat16)
    rhs_wide[ranks : ranks + wide, 0:span] = jnp.zeros((wide, span), jnp.bfloat16)
    rhs_wide[ranks : ranks + wide, span : 2 * span] = spread.astype(jnp.bfloat16)
    rhs_back[0:span, :] = jnp.concatenate([time_all, time_zero], axis=0).T.astype(jnp.bfloat16)
    rhs_back[span : 2 * span, :] = jnp.concatenate([time_zero, time_all], axis=0).T.astype(jnp.bfloat16)
    time_part[...] = jnp.zeros_like(time_part)

    def pair_copy(s, j):
        return pltpu.make_async_remote_copy(
            src_ref=parts.at[s, 2 * j + 1 - core], dst_ref=pair.at[s, j],
            send_sem=pair_send.at[s, j], recv_sem=pair_recv.at[s, j],
            device_id=(f, partner), device_id_type=MESH,
        )

    def sum_copy(s, j, slot):
        target = (xor(my_chunk, steps - 1 - s, steps) * pairs + j) * 2 + core
        return pltpu.make_async_remote_copy(
            src_ref=sums.at[s, j], dst_ref=landed.at[s, slot],
            send_sem=sum_send.at[s, j], recv_sem=sum_recv.at[s, slot],
            device_id=(f, target), device_id_type=MESH,
        )

    def halo_copy(index):
        distance, place, slot, count = pieces[index]
        return pltpu.make_async_remote_copy(
            src_ref=time_ref.at[band_rows, pl.ds(place * LANES, count * LANES)],
            dst_ref=window.at[:, pl.ds(slot * LANES, count * LANES)],
            send_sem=halo_send.at[index], recv_sem=halo_recv.at[index],
            device_id=(f, (tm - distance + tms) % tms), device_id_type=MESH,
        )

    def halo_goes(index):
        to = tm - pieces[index][0]
        return jnp.logical_and(to >= 0, to < tms)

    def halo_comes(index):
        source = tm + pieces[index][0]
        return jnp.logical_and(source >= 0, source < tms)

    def time_copy(k):
        peer = (f + k) % feeders
        return pltpu.make_async_remote_copy(
            src_ref=time_part.at[pl.ds(pl.multiple_of(peer * band, 8), band), :],
            dst_ref=time_landed.at[k - 1],
            send_sem=time_send.at[k - 1], recv_sem=time_recv.at[k - 1],
            device_id=(peer, tm), device_id_type=MESH,
        )

    def forward(s):
        for j in range(pairs):
            pair_copy(s, j).wait_recv()
            sums[s, j] = parts[s, 2 * j + core] + pair[s, j]
            sum_copy(s, j, my_pair).start()

    def step(s, carry):
        for copy in loads(s):
            copy.wait()
        factor_t = factor[s]
        both = jnp.concatenate([factor_t, words[s].astype(jnp.float32)], axis=0).T.astype(jnp.bfloat16)
        product = jnp.dot(both, rhs_wide[...], preferred_element_type=jnp.float32)
        bits = jnp.bitwise_and(product[:, span:].astype(jnp.int32), 1)
        exact = jnp.where(bits == 1, product[:, :span] - obs[s].astype(jnp.float32), 0.0)
        residual = exact.astype(jnp.bfloat16)
        cut = residual if half % 16 == 0 else exact
        left = jnp.concatenate([cut[d * share : d * share + half] for d in range(members)], axis=0)
        right = jnp.concatenate([cut[d * share + half : (d + 1) * share] for d in range(members)], axis=0)
        stacked = jnp.concatenate([left, right], axis=1).astype(jnp.bfloat16)
        grads = jnp.dot(stacked, rhs_back[...], preferred_element_type=jnp.float32)
        for d in range(members):
            parts[s, d] = grads[d * half : (d + 1) * half]
        time_part[...] += jnp.dot(factor_t.astype(jnp.bfloat16), residual, preferred_element_type=jnp.float32)

        @pl.when(s == 0)
        def _():
            pl.semaphore_wait(barrier, tms - 1 + feeders - 1)
            for index in range(len(pieces)):
                @pl.when(halo_goes(index))
                def _(index=index):
                    halo_copy(index).start()

        for j in range(pairs):
            pair_copy(s, j).start()

        @pl.when(s >= 1)
        def _():
            forward(s - 1)

        return carry

    lax.fori_loop(0, steps, step, 0)
    last = steps - 1
    for k in range(1, feeders):
        time_copy(k).start()

    time_own = time_ref[band_rows, :]
    for index in range(len(pieces)):
        @pl.when(halo_comes(index))
        def _(index=index):
            halo_copy(index).wait_recv()

    third = slots // 3 * LANES
    own_at = third + LANES
    window[:, own_at : own_at + span] = time_own
    weights[...] = jnp.zeros_like(weights)
    lag_count = weight_ref.shape[0]
    weights[0:ranks, 0:lag_count] = weight_ref[...].T
    weight = weights[band_rows, :]
    far = -(-LAGMAX // LANES)
    ahead = far * LANES - LAGMAX
    errors_width = span + LANES
    past = window[:, 0:third]
    mid = window[:, third : 2 * third]
    future = window[:, 2 * third : 3 * third]
    short, shifts = [], []
    long = jnp.zeros((band, 1), jnp.float32)
    for index in range(lag_count):
        lag = lags_ref[index]
        here = weight[:, index : index + 1]
        is_long = lag >= LANES
        short.append(jnp.where(is_long, 0.0, here))
        long = long + jnp.where(is_long, here, 0.0)
        shifts.append(jnp.where(is_long, 0, lag))
    near = long * pltpu.roll(past, third - ahead, 1)[:, 0:errors_width]
    later = long * pltpu.roll(mid, third - ahead, 1)[:, 0:errors_width]
    for index in range(lag_count):
        near = near + short[index] * pltpu.roll(mid, shifts[index], 1)[:, LANES:]
        later = later + short[index] * pltpu.roll(future, shifts[index], 1)[:, LANES:]
    columns = lax.broadcasted_iota(jnp.int32, (band, errors_width), 1) + tm * span
    errors = jnp.where(
        jnp.logical_and(columns >= LAGMAX, columns < tms * span), mid[:, LANES:] - near, 0.0
    )
    later_columns = columns + (far - 1) * LANES
    later_errors = jnp.where(
        jnp.logical_and(later_columns >= LAGMAX, later_columns < tms * span), future[:, LANES:] - later, 0.0
    )
    carried = long * pltpu.roll(later_errors, errors_width - (LANES - ahead), 1)[:, 0:span]
    for index in range(lag_count):
        carried = carried + short[index] * pltpu.roll(errors, errors_width - shifts[index], 1)[:, 0:span]
    adjoint = errors[:, 0:span] - carried
    regular = LAM_AR * adjoint + LAM_X * time_own

    for j in range(pairs):
        pair_copy(last, j).wait_recv()
        sums[last, j] = parts[last, 2 * j + core] + pair[last, j]
        if pairs > 1:
            @pl.when(j != my_pair)
            def _(j=j):
                sum_copy(last, j, my_pair).start()

    total = sums[last, my_pair]
    for s in range(steps):
        for j in range(pairs):
            if s < last:
                sum_copy(s, j, j).wait_recv()
                total = total + landed[s, j]
            elif pairs > 1:
                @pl.when(j != my_pair)
                def _(j=j):
                    sum_copy(last, j, j).wait_recv()

                total = total + jnp.where(j == my_pair, 0.0, landed[last, j])
    turned = total.T
    gradient = jnp.concatenate([turned[0:ranks], turned[ranks : 2 * ranks]], axis=1)
    own_chunk = factor[last]
    own = own_chunk[:, 0:share]
    for d in range(1, members):
        own = jnp.where(tm % members == d, own_chunk[:, d * share : (d + 1) * share], own)
    gradient = DATA_WEIGHT * gradient + LAM_F * own
    new_first = BETA_ONE * first_ref[...] + (1.0 - BETA_ONE) * gradient
    new_second = BETA_TWO * second_ref[...] + (1.0 - BETA_TWO) * gradient * gradient
    update = (
        LEARNING_RATE * (new_first / BIAS_FIRST) / (jnp.sqrt(new_second / BIAS_SECOND) + ADAM_EPS)
    )
    new_first_ref[...] = new_first
    new_second_ref[...] = new_second
    new_factor_ref[...] = own - update

    data = time_part[band_rows, :]
    for k in range(1, feeders):
        time_copy(k).wait_recv()
        data = data + time_landed[k - 1]
    time_grad_ref[...] = DATA_WEIGHT * data + regular

    for index in range(len(pieces)):
        @pl.when(halo_goes(index))
        def _(index=index):
            halo_copy(index).wait_send()

    for k in range(1, feeders):
        time_copy(k).wait_send()
    for s in range(steps):
        for j in range(pairs):
            pair_copy(s, j).wait_send()
            if s < last:
                sum_copy(s, j, my_pair).wait_send()
            elif pairs > 1:
                @pl.when(j != my_pair)
                def _(s=s, j=j):
                    sum_copy(s, j, my_pair).wait_send()


def per_device(
    observed, mask_words, feeder_factor, time_factor, ar_weight, lags, moment_first, moment_second
):
    rows, span = observed.shape
    ranks = time_factor.shape[0]
    tms = lax.axis_size("tm")
    feeders = lax.axis_size("feeder")
    share = rows // tms
    members = 2
    while members * share % LANES:
        members *= 2
    chunk = members * share
    steps = rows // chunk
    pairs = members // 2
    half = share // 2
    band = ranks // feeders
    pieces, slots = halo_pieces(span)
    f32 = jnp.float32
    block = (half, 2 * ranks)
    dma = pltpu.SemaphoreType.DMA
    vmem = pl.BlockSpec(memory_space=pltpu.VMEM)
    hbm = pl.BlockSpec(memory_space=pl.ANY)
    flops = 2 * rows * span * ranks * 4
    new_factor, new_first, new_second, time_grad = pl.pallas_call(
        functools.partial(kernel, feeders, tms, chunk, share),
        out_shape=[jax.ShapeDtypeStruct((ranks, share), f32)] * 3
        + [jax.ShapeDtypeStruct((band, span), f32)],
        in_specs=[hbm, hbm, hbm, vmem, vmem, pl.BlockSpec(memory_space=pltpu.SMEM), vmem, vmem],
        out_specs=[vmem] * 4,
        scratch_shapes=[
            pltpu.VMEM((steps, chunk, span), jnp.bfloat16),
            pltpu.VMEM((steps, span // 8, chunk), jnp.int32),
            pltpu.VMEM((steps, ranks, chunk), f32),
            pltpu.VMEM((ranks + span // 8, 2 * span), jnp.bfloat16),
            pltpu.VMEM((2 * span, 2 * ranks), jnp.bfloat16),
            pltpu.VMEM((band, slots * LANES), f32),
            pltpu.VMEM((ranks, LANES), f32),
            pltpu.VMEM((steps, members) + block, f32),
            pltpu.VMEM((steps, pairs) + block, f32),
            pltpu.VMEM((steps, pairs) + block, f32),
            pltpu.VMEM((steps, pairs) + block, f32),
            pltpu.VMEM((ranks, span), f32),
            pltpu.VMEM((feeders - 1, band, span), f32),
            dma((3, steps)),
            dma((steps, pairs)),
            dma((steps, pairs)),
            dma((steps, pairs)),
            dma((steps, pairs)),
            dma((feeders - 1,)),
            dma((feeders - 1,)),
            dma((len(pieces),)),
            dma((len(pieces),)),
        ],
        compiler_params=pltpu.CompilerParams(
            collective_id=0, has_side_effects=True, vmem_limit_bytes=40 * 1024 * 1024
        ),
        cost_estimate=pl.CostEstimate(flops=flops, bytes_accessed=rows * span * 3, transcendentals=0),
    )(
        observed, mask_words.T, feeder_factor.T, time_factor, ar_weight, lags,
        moment_first.T, moment_second.T,
    )
    return (new_factor.T, new_first.T, new_second.T, time_grad)


def solution(mesh):
    placed = (
        P("feeder", "tm"),
        P("feeder", "tm"),
        P("feeder", None),
        P(None, "tm"),
        P(),
        P(),
        P(("feeder", "tm"), None),
        P(("feeder", "tm"), None),
    )
    return jax.shard_map(
        per_device,
        mesh=mesh,
        in_specs=placed,
        out_specs=(
            P(("feeder", "tm"), None),
            P(("feeder", "tm"), None),
            P(("feeder", "tm"), None),
            P("feeder", "tm"),
        ),
        check_vma=False,
    )
```

```python
import functools

import jax
import jax.numpy as jnp
from jax import lax
from jax.experimental import pallas as pl
from jax.experimental.pallas import tpu as pltpu
from jax.sharding import PartitionSpec as P

LAGMAX = 1440
LANES = 128
MESH = pl.DeviceIdType.MESH

DATA_WEIGHT = 1.0 / 64.0
LAM_F = 0.1
LAM_X = 0.01
LAM_AR = 8.0
BETA_ONE = 0.9
BETA_TWO = 0.999
BIAS_FIRST = 1.0 - 0.9**8
BIAS_SECOND = 1.0 - 0.999**8
LEARNING_RATE = 0.05
ADAM_EPS = 1e-08


def xor(a, b, count):
    total = 0
    bit = 1
    while bit < count:
        total = total + bit * ((a // bit + b // bit) % 2)
        bit *= 2
    return total


def halo_pieces(span):
    blocks = span // LANES
    far = -(-LAGMAX // LANES)
    wanted = (
        list(range(-far, blocks + 2 - far))
        + list(range(-1, blocks + 1))
        + list(range(far - 2, far + blocks))
    )
    pieces = []
    for slot, block in enumerate(wanted):
        distance, place = divmod(block, blocks)
        if distance == 0:
            continue
        last = pieces[-1] if pieces else None
        if last and last[0] == distance and last[1] + last[3] == place and last[2] + last[3] == slot:
            last[3] += 1
        else:
            pieces.append([distance, place, slot, 1])
    return pieces, len(wanted)


def kernel(
    feeders, tms, chunk, share,
    obs_hbm, words_hbm, factor_hbm, time_hbm, weight_hbm, lags_ref, first_hbm, second_hbm,
    new_factor_ref, new_first_ref, new_second_ref, time_grad_ref,
    obs, words, factor, time_ref, weight_ref, first_ref, second_ref, rhs_wide, rhs_back, window, weights,
    parts, pair, sums, landed, time_part, time_landed,
    in_sem, small_sem, pair_send, pair_recv, sum_send, sum_recv, time_send, time_recv, halo_send, halo_recv,
):
    ranks, span = time_ref.shape
    rows = obs_hbm.shape[0]
    steps = rows // chunk
    members = chunk // share
    pairs = members // 2
    half = share // 2
    band = ranks // feeders
    f = lax.axis_index("feeder")
    tm = lax.axis_index("tm")
    core = tm % 2
    my_chunk = tm // members
    my_pair = (tm // 2) % pairs
    partner = tm + 1 - 2 * core
    band_rows = pl.ds(pl.multiple_of(f * band, 8), band)
    pieces, slots = halo_pieces(span)
    blocks = span // LANES

    def loads(s):
        start = pl.multiple_of(xor(my_chunk, steps - 1 - s, steps) * chunk, LANES)
        where = pl.ds(start, chunk)
        return (
            pltpu.make_async_copy(obs_hbm.at[where, :], obs.at[s], in_sem.at[0, s]),
            pltpu.make_async_copy(words_hbm.at[:, where], words.at[s], in_sem.at[1, s]),
            pltpu.make_async_copy(factor_hbm.at[:, where], factor.at[s], in_sem.at[2, s]),
        )

    time_load, weight_load, first_load, second_load = [
        pltpu.make_async_copy(source, target, small_sem.at[index])
        for index, (source, target) in enumerate(
            [(time_hbm, time_ref), (weight_hbm, weight_ref), (first_hbm, first_ref), (second_hbm, second_ref)]
        )
    ]
    time_load.start()
    for s in range(steps):
        for copy in loads(s):
            copy.start()
    for copy in (weight_load, first_load, second_load):
        copy.start()

    window[...] = jnp.zeros_like(window)
    barrier = pltpu.get_barrier_semaphore()

    @pl.loop(1, tms)
    def _(k):
        pl.semaphore_signal(barrier, inc=1, device_id=(f, (tm + k) % tms), device_id_type=MESH)

    for k in range(1, feeders):
        pl.semaphore_signal(barrier, inc=1, device_id=((f + k) % feeders, tm), device_id_type=MESH)

    time_load.wait()
    time_all = time_ref[...]
    time_zero = jnp.zeros_like(time_all)
    wide = span // 8
    column = lax.broadcasted_iota(jnp.int32, (wide, span), 1)
    word = lax.broadcasted_iota(jnp.int32, (wide, span), 0)
    level = jnp.left_shift(jnp.int32(1), 7 - jnp.bitwise_and(column, 7)).astype(jnp.float32) * (1.0 / 128.0)
    spread = jnp.where(jnp.right_shift(column, 3) == word, level, 0.0)
    rhs_wide[0:ranks, 0:span] = time_all.astype(jnp.bfloat16)
    rhs_wide[0:ranks, span : 2 * span] = jnp.zeros((ranks, span), jnp.bfloat16)
    rhs_wide[ranks : ranks + wide, 0:span] = jnp.zeros((wide, span), jnp.bfloat16)
    rhs_wide[ranks : ranks + wide, span : 2 * span] = spread.astype(jnp.bfloat16)
    rhs_back[0:span, :] = jnp.concatenate([time_all, time_zero], axis=0).T.astype(jnp.bfloat16)
    rhs_back[span : 2 * span, :] = jnp.concatenate([time_zero, time_all], axis=0).T.astype(jnp.bfloat16)
    time_part[...] = jnp.zeros_like(time_part)

    def pair_copy(s, j):
        return pltpu.make_async_remote_copy(
            src_ref=parts.at[s, 2 * j + 1 - core], dst_ref=pair.at[s, j],
            send_sem=pair_send.at[s, j], recv_sem=pair_recv.at[s, j],
            device_id=(f, partner), device_id_type=MESH,
        )

    def sum_copy(s, j, slot):
        target = (xor(my_chunk, steps - 1 - s, steps) * pairs + j) * 2 + core
        return pltpu.make_async_remote_copy(
            src_ref=sums.at[s, j], dst_ref=landed.at[s, slot],
            send_sem=sum_send.at[s, j], recv_sem=sum_recv.at[s, slot],
            device_id=(f, target), device_id_type=MESH,
        )

    def halo_copy(index):
        distance, place, slot, count = pieces[index]
        return pltpu.make_async_remote_copy(
            src_ref=time_ref.at[band_rows, pl.ds(place * LANES, count * LANES)],
            dst_ref=window.at[:, pl.ds(slot * LANES, count * LANES)],
            send_sem=halo_send.at[index], recv_sem=halo_recv.at[index],
            device_id=(f, (tm - distance + tms) % tms), device_id_type=MESH,
        )

    def halo_goes(index):
        to = tm - pieces[index][0]
        return jnp.logical_and(to >= 0, to < tms)

    def halo_comes(index):
        source = tm + pieces[index][0]
        return jnp.logical_and(source >= 0, source < tms)

    def time_copy(k):
        peer = (f + k) % feeders
        return pltpu.make_async_remote_copy(
            src_ref=time_part.at[pl.ds(pl.multiple_of(peer * band, 8), band), :],
            dst_ref=time_landed.at[k - 1],
            send_sem=time_send.at[k - 1], recv_sem=time_recv.at[k - 1],
            device_id=(peer, tm), device_id_type=MESH,
        )

    def forward(s):
        for j in range(pairs):
            pair_copy(s, j).wait_recv()
            sums[s, j] = parts[s, 2 * j + core] + pair[s, j]
            sum_copy(s, j, my_pair).start()

    def step(s, carry):
        for copy in loads(s):
            copy.wait()
        factor_t = factor[s]
        both = jnp.concatenate([factor_t, words[s].astype(jnp.float32)], axis=0).T.astype(jnp.bfloat16)
        product = jnp.dot(both, rhs_wide[...], preferred_element_type=jnp.float32)
        bits = jnp.bitwise_and(product[:, span:].astype(jnp.int32), 1)
        exact = jnp.where(bits == 1, product[:, :span] - obs[s].astype(jnp.float32), 0.0)
        residual = exact.astype(jnp.bfloat16)
        cut = residual if half % 16 == 0 else exact
        left = jnp.concatenate([cut[d * share : d * share + half] for d in range(members)], axis=0)
        right = jnp.concatenate([cut[d * share + half : (d + 1) * share] for d in range(members)], axis=0)
        stacked = jnp.concatenate([left, right], axis=1).astype(jnp.bfloat16)
        grads = jnp.dot(stacked, rhs_back[...], preferred_element_type=jnp.float32)
        for d in range(members):
            parts[s, d] = grads[d * half : (d + 1) * half]
        time_part[...] += jnp.dot(factor_t.astype(jnp.bfloat16), residual, preferred_element_type=jnp.float32)

        @pl.when(s == 0)
        def _():
            pl.semaphore_wait(barrier, tms - 1 + feeders - 1)
            for index in range(len(pieces)):
                @pl.when(halo_goes(index))
                def _(index=index):
                    halo_copy(index).start()

        for j in range(pairs):
            pair_copy(s, j).start()

        @pl.when(s >= 1)
        def _():
            forward(s - 1)

        return carry

    lax.fori_loop(0, steps, step, 0)
    last = steps - 1
    for k in range(1, feeders):
        time_copy(k).start()

    time_own = time_ref[band_rows, :]
    for index in range(len(pieces)):
        @pl.when(halo_comes(index))
        def _(index=index):
            halo_copy(index).wait_recv()

    third = slots // 3 * LANES
    own_at = third + LANES
    window[:, own_at : own_at + span] = time_own
    weight_load.wait()
    weights[...] = jnp.zeros_like(weights)
    lag_count = weight_ref.shape[0]
    weights[0:ranks, 0:lag_count] = weight_ref[...].T
    weight = weights[band_rows, :]
    far = -(-LAGMAX // LANES)
    ahead = far * LANES - LAGMAX
    errors_width = span + LANES
    past = window[:, 0:third]
    mid = window[:, third : 2 * third]
    future = window[:, 2 * third : 3 * third]
    short, shifts = [], []
    long = jnp.zeros((band, 1), jnp.float32)
    for index in range(lag_count):
        lag = lags_ref[index]
        here = weight[:, index : index + 1]
        is_long = lag >= LANES
        short.append(jnp.where(is_long, 0.0, here))
        long = long + jnp.where(is_long, here, 0.0)
        shifts.append(jnp.where(is_long, 0, lag))
    near = long * pltpu.roll(past, third - ahead, 1)[:, 0:errors_width]
    later = long * pltpu.roll(mid, third - ahead, 1)[:, 0:errors_width]
    for index in range(lag_count):
        near = near + short[index] * pltpu.roll(mid, shifts[index], 1)[:, LANES:]
        later = later + short[index] * pltpu.roll(future, shifts[index], 1)[:, LANES:]
    columns = lax.broadcasted_iota(jnp.int32, (band, errors_width), 1) + tm * span
    errors = jnp.where(
        jnp.logical_and(columns >= LAGMAX, columns < tms * span), mid[:, LANES:] - near, 0.0
    )
    later_columns = columns + (far - 1) * LANES
    later_errors = jnp.where(
        jnp.logical_and(later_columns >= LAGMAX, later_columns < tms * span), future[:, LANES:] - later, 0.0
    )
    carried = long * pltpu.roll(later_errors, errors_width - (LANES - ahead), 1)[:, 0:span]
    for index in range(lag_count):
        carried = carried + short[index] * pltpu.roll(errors, errors_width - shifts[index], 1)[:, 0:span]
    adjoint = errors[:, 0:span] - carried
    regular = LAM_AR * adjoint + LAM_X * time_own

    for j in range(pairs):
        pair_copy(last, j).wait_recv()
        sums[last, j] = parts[last, 2 * j + core] + pair[last, j]
        if pairs > 1:
            @pl.when(j != my_pair)
            def _(j=j):
                sum_copy(last, j, my_pair).start()

    total = sums[last, my_pair]
    for s in range(steps):
        for j in range(pairs):
            if s < last:
                sum_copy(s, j, j).wait_recv()
                total = total + landed[s, j]
            elif pairs > 1:
                @pl.when(j != my_pair)
                def _(j=j):
                    sum_copy(last, j, j).wait_recv()

                total = total + jnp.where(j == my_pair, 0.0, landed[last, j])
    turned = total.T
    gradient = jnp.concatenate([turned[0:ranks], turned[ranks : 2 * ranks]], axis=1)
    own_chunk = factor[last]
    own = own_chunk[:, 0:share]
    for d in range(1, members):
        own = jnp.where(tm % members == d, own_chunk[:, d * share : (d + 1) * share], own)
    gradient = DATA_WEIGHT * gradient + LAM_F * own
    first_load.wait()
    second_load.wait()
    new_first = BETA_ONE * first_ref[...] + (1.0 - BETA_ONE) * gradient
    new_second = BETA_TWO * second_ref[...] + (1.0 - BETA_TWO) * gradient * gradient
    update = (
        LEARNING_RATE * (new_first / BIAS_FIRST) / (jnp.sqrt(new_second / BIAS_SECOND) + ADAM_EPS)
    )
    new_first_ref[...] = new_first
    new_second_ref[...] = new_second
    new_factor_ref[...] = own - update

    data = time_part[band_rows, :]
    for k in range(1, feeders):
        time_copy(k).wait_recv()
        data = data + time_landed[k - 1]
    time_grad_ref[...] = DATA_WEIGHT * data + regular

    for index in range(len(pieces)):
        @pl.when(halo_goes(index))
        def _(index=index):
            halo_copy(index).wait_send()

    for k in range(1, feeders):
        time_copy(k).wait_send()
    for s in range(steps):
        for j in range(pairs):
            pair_copy(s, j).wait_send()
            if s < last:
                sum_copy(s, j, my_pair).wait_send()
            elif pairs > 1:
                @pl.when(j != my_pair)
                def _(s=s, j=j):
                    sum_copy(s, j, my_pair).wait_send()


def hand_over(a, b, c, d, a_out, b_out, c_out, d_out, sem):
    copies = [
        pltpu.make_async_copy(source, target, sem.at[index])
        for index, (source, target) in enumerate([(a, a_out), (b, b_out), (c, c_out), (d, d_out)])
    ]
    for copy in copies:
        copy.start()
    for copy in copies:
        copy.wait()


def per_device(
    observed, mask_words, feeder_factor, time_factor, ar_weight, lags, moment_first, moment_second
):
    rows, span = observed.shape
    ranks = time_factor.shape[0]
    tms = lax.axis_size("tm")
    feeders = lax.axis_size("feeder")
    share = rows // tms
    members = 2
    while members * share % LANES:
        members *= 2
    chunk = members * share
    steps = rows // chunk
    pairs = members // 2
    half = share // 2
    band = ranks // feeders
    pieces, slots = halo_pieces(span)
    f32 = jnp.float32
    block = (half, 2 * ranks)
    dma = pltpu.SemaphoreType.DMA
    vmem = pl.BlockSpec(memory_space=pltpu.VMEM)
    hbm = pl.BlockSpec(memory_space=pl.ANY)
    flops = 2 * rows * span * ranks * 4
    results = pl.pallas_call(
        functools.partial(kernel, feeders, tms, chunk, share),
        out_shape=[jax.ShapeDtypeStruct((ranks, share), f32)] * 3
        + [jax.ShapeDtypeStruct((band, span), f32)],
        in_specs=[hbm, hbm, hbm, hbm, hbm, pl.BlockSpec(memory_space=pltpu.SMEM), hbm, hbm],
        out_specs=[vmem] * 4,
        scratch_shapes=[
            pltpu.VMEM((steps, chunk, span), jnp.bfloat16),
            pltpu.VMEM((steps, span // 8, chunk), jnp.int32),
            pltpu.VMEM((steps, ranks, chunk), f32),
            pltpu.VMEM((ranks, span), f32),
            pltpu.VMEM(ar_weight.shape, f32),
            pltpu.VMEM((ranks, share), f32),
            pltpu.VMEM((ranks, share), f32),
            pltpu.VMEM((ranks + span // 8, 2 * span), jnp.bfloat16),
            pltpu.VMEM((2 * span, 2 * ranks), jnp.bfloat16),
            pltpu.VMEM((band, slots * LANES), f32),
            pltpu.VMEM((ranks, LANES), f32),
            pltpu.VMEM((steps, members) + block, f32),
            pltpu.VMEM((steps, pairs) + block, f32),
            pltpu.VMEM((steps, pairs) + block, f32),
            pltpu.VMEM((steps, pairs) + block, f32),
            pltpu.VMEM((ranks, span), f32),
            pltpu.VMEM((feeders - 1, band, span), f32),
            dma((3, steps)),
            dma((4,)),
            dma((steps, pairs)),
            dma((steps, pairs)),
            dma((steps, pairs)),
            dma((steps, pairs)),
            dma((feeders - 1,)),
            dma((feeders - 1,)),
            dma((len(pieces),)),
            dma((len(pieces),)),
        ],
        compiler_params=pltpu.CompilerParams(
            collective_id=0, has_side_effects=True, vmem_limit_bytes=63 * 1024 * 1024
        ),
        cost_estimate=pl.CostEstimate(flops=flops, bytes_accessed=rows * span * 3, transcendentals=0),
    )(
        observed, mask_words.T, feeder_factor.T, time_factor, ar_weight, lags,
        moment_first.T, moment_second.T,
    )
    new_factor, new_first, new_second, time_grad = pl.pallas_call(
        hand_over,
        out_shape=[jax.ShapeDtypeStruct(result.shape, f32) for result in results],
        in_specs=[hbm] * 4,
        out_specs=[hbm] * 4,
        scratch_shapes=[dma((4,))],
    )(*results)
    return (new_factor.T, new_first.T, new_second.T, time_grad)


def solution(mesh):
    placed = (
        P("feeder", "tm"),
        P("feeder", "tm"),
        P("feeder", None),
        P(None, "tm"),
        P(),
        P(),
        P(("feeder", "tm"), None),
        P(("feeder", "tm"), None),
    )
    return jax.shard_map(
        per_device,
        mesh=mesh,
        in_specs=placed,
        out_specs=(
            P(("feeder", "tm"), None),
            P(("feeder", "tm"), None),
            P(("feeder", "tm"), None),
            P("feeder", "tm"),
        ),
        check_vma=False,
    )
```

```python
import functools

import jax
import jax.numpy as jnp
from jax import lax
from jax.experimental import pallas as pl
from jax.experimental.pallas import tpu as pltpu
from jax.sharding import PartitionSpec as P

LAGMAX = 1440
LANES = 128
MESH = pl.DeviceIdType.MESH

DATA_WEIGHT = 1.0 / 64.0
LAM_F = 0.1
LAM_X = 0.01
LAM_AR = 8.0
BETA_ONE = 0.9
BETA_TWO = 0.999
BIAS_FIRST = 1.0 - 0.9**8
BIAS_SECOND = 1.0 - 0.999**8
LEARNING_RATE = 0.05
ADAM_EPS = 1e-08


def xor(a, b, count):
    total = 0
    bit = 1
    while bit < count:
        total = total + bit * ((a // bit + b // bit) % 2)
        bit *= 2
    return total


def halo_pieces(span):
    blocks = span // LANES
    far = -(-LAGMAX // LANES)
    wanted = (
        list(range(-far, blocks + 2 - far))
        + list(range(-1, blocks + 1))
        + list(range(far - 2, far + blocks))
    )
    pieces = []
    for slot, block in enumerate(wanted):
        distance, place = divmod(block, blocks)
        if distance == 0:
            continue
        last = pieces[-1] if pieces else None
        if last and last[0] == distance and last[1] + last[3] == place and last[2] + last[3] == slot:
            last[3] += 1
        else:
            pieces.append([distance, place, slot, 1])
    return pieces, len(wanted)


def kernel(
    feeders, tms, chunk, share,
    obs_hbm, words_hbm, factor_hbm, time_hbm, weight_hbm, lags_ref, first_hbm, second_hbm,
    new_factor_ref, new_first_ref, new_second_ref, time_grad_ref,
    obs, words, factor, time_ref, weight_ref, first_ref, second_ref, rhs_wide, rhs_back, window, weights,
    parts, pair, sums, landed, time_part, time_landed,
    in_sem, small_sem, pair_send, pair_recv, sum_send, sum_recv, time_send, time_recv, halo_send, halo_recv,
):
    ranks, span = time_ref.shape
    rows = obs_hbm.shape[0]
    steps = rows // chunk
    members = chunk // share
    pairs = members // 2
    half = share // 2
    band = ranks // feeders
    f = lax.axis_index("feeder")
    tm = lax.axis_index("tm")
    core = tm % 2
    my_chunk = tm // members
    my_pair = (tm // 2) % pairs
    partner = tm + 1 - 2 * core
    band_rows = pl.ds(pl.multiple_of(f * band, 8), band)
    pieces, slots = halo_pieces(span)
    blocks = span // LANES

    def loads(s):
        start = pl.multiple_of(xor(my_chunk, steps - 1 - s, steps) * chunk, LANES)
        where = pl.ds(start, chunk)
        return (
            pltpu.make_async_copy(obs_hbm.at[where, :], obs.at[s], in_sem.at[0, s]),
            pltpu.make_async_copy(words_hbm.at[:, where], words.at[s], in_sem.at[1, s]),
            pltpu.make_async_copy(factor_hbm.at[:, where], factor.at[s], in_sem.at[2, s]),
        )

    time_load, weight_load, first_load, second_load = [
        pltpu.make_async_copy(source, target, small_sem.at[index])
        for index, (source, target) in enumerate(
            [(time_hbm, time_ref), (weight_hbm, weight_ref), (first_hbm, first_ref), (second_hbm, second_ref)]
        )
    ]
    time_load.start()
    for s in range(steps):
        for copy in loads(s):
            copy.start()
    for copy in (weight_load, first_load, second_load):
        copy.start()

    window[...] = jnp.zeros_like(window)
    barrier = pltpu.get_barrier_semaphore()

    @pl.loop(1, tms)
    def _(k):
        pl.semaphore_signal(barrier, inc=1, device_id=(f, (tm + k) % tms), device_id_type=MESH)

    for k in range(1, feeders):
        pl.semaphore_signal(barrier, inc=1, device_id=((f + k) % feeders, tm), device_id_type=MESH)

    time_load.wait()
    time_all = time_ref[...]
    time_zero = jnp.zeros_like(time_all)
    wide = span // 8
    column = lax.broadcasted_iota(jnp.int32, (wide, span), 1)
    word = lax.broadcasted_iota(jnp.int32, (wide, span), 0)
    level = jnp.left_shift(jnp.int32(1), 7 - jnp.bitwise_and(column, 7)).astype(jnp.float32) * (1.0 / 128.0)
    spread = jnp.where(jnp.right_shift(column, 3) == word, level, 0.0)
    rhs_wide[0:ranks, 0:span] = time_all.astype(jnp.bfloat16)
    rhs_wide[0:ranks, span : 2 * span] = jnp.zeros((ranks, span), jnp.bfloat16)
    rhs_wide[ranks : ranks + wide, 0:span] = jnp.zeros((wide, span), jnp.bfloat16)
    rhs_wide[ranks : ranks + wide, span : 2 * span] = spread.astype(jnp.bfloat16)
    rhs_back[0:span, :] = jnp.concatenate([time_all, time_zero], axis=0).T.astype(jnp.bfloat16)
    rhs_back[span : 2 * span, :] = jnp.concatenate([time_zero, time_all], axis=0).T.astype(jnp.bfloat16)
    time_part[...] = jnp.zeros_like(time_part)

    def pair_copy(s, j):
        return pltpu.make_async_remote_copy(
            src_ref=parts.at[s, 2 * j + 1 - core], dst_ref=pair.at[s, j],
            send_sem=pair_send.at[s, j], recv_sem=pair_recv.at[s, j],
            device_id=(f, partner), device_id_type=MESH,
        )

    def sum_copy(s, j, slot):
        target = (xor(my_chunk, steps - 1 - s, steps) * pairs + j) * 2 + core
        return pltpu.make_async_remote_copy(
            src_ref=sums.at[s, j], dst_ref=landed.at[s, slot],
            send_sem=sum_send.at[s, j], recv_sem=sum_recv.at[s, slot],
            device_id=(f, target), device_id_type=MESH,
        )

    def halo_copy(index):
        distance, place, slot, count = pieces[index]
        return pltpu.make_async_remote_copy(
            src_ref=time_ref.at[band_rows, pl.ds(place * LANES, count * LANES)],
            dst_ref=window.at[:, pl.ds(slot * LANES, count * LANES)],
            send_sem=halo_send.at[index], recv_sem=halo_recv.at[index],
            device_id=(f, (tm - distance + tms) % tms), device_id_type=MESH,
        )

    def halo_goes(index):
        to = tm - pieces[index][0]
        return jnp.logical_and(to >= 0, to < tms)

    def halo_comes(index):
        source = tm + pieces[index][0]
        return jnp.logical_and(source >= 0, source < tms)

    def time_copy(k):
        peer = (f + k) % feeders
        return pltpu.make_async_remote_copy(
            src_ref=time_part.at[pl.ds(pl.multiple_of(peer * band, 8), band), :],
            dst_ref=time_landed.at[k - 1],
            send_sem=time_send.at[k - 1], recv_sem=time_recv.at[k - 1],
            device_id=(peer, tm), device_id_type=MESH,
        )

    def forward(s):
        for j in range(pairs):
            pair_copy(s, j).wait_recv()
            sums[s, j] = parts[s, 2 * j + core] + pair[s, j]
            sum_copy(s, j, my_pair).start()

    def step(s, carry):
        for copy in loads(s):
            copy.wait()
        factor_t = factor[s]
        both = jnp.concatenate([factor_t, words[s].astype(jnp.float32)], axis=0).T.astype(jnp.bfloat16)
        product = jnp.dot(both, rhs_wide[...], preferred_element_type=jnp.float32)
        bits = jnp.bitwise_and(product[:, span:].astype(jnp.int32), 1)
        exact = jnp.where(bits == 1, product[:, :span] - obs[s].astype(jnp.float32), 0.0)
        residual = exact.astype(jnp.bfloat16)
        cut = residual if half % 16 == 0 else exact
        left = jnp.concatenate([cut[d * share : d * share + half] for d in range(members)], axis=0)
        right = jnp.concatenate([cut[d * share + half : (d + 1) * share] for d in range(members)], axis=0)
        stacked = jnp.concatenate([left, right], axis=1).astype(jnp.bfloat16)
        grads = jnp.dot(stacked, rhs_back[...], preferred_element_type=jnp.float32)
        for d in range(members):
            parts[s, d] = grads[d * half : (d + 1) * half]
        time_part[...] += jnp.dot(factor_t.astype(jnp.bfloat16), residual, preferred_element_type=jnp.float32)

        @pl.when(s == 0)
        def _():
            pl.semaphore_wait(barrier, tms - 1 + feeders - 1)
            for index in range(len(pieces)):
                @pl.when(halo_goes(index))
                def _(index=index):
                    halo_copy(index).start()

        for j in range(pairs):
            pair_copy(s, j).start()

        @pl.when(s >= 1)
        def _():
            forward(s - 1)

        return carry

    lax.fori_loop(0, steps, step, 0)
    last = steps - 1
    for k in range(1, feeders):
        time_copy(k).start()

    time_own = time_ref[band_rows, :]
    for index in range(len(pieces)):
        @pl.when(halo_comes(index))
        def _(index=index):
            halo_copy(index).wait_recv()

    third = slots // 3 * LANES
    own_at = third + LANES
    window[:, own_at : own_at + span] = time_own
    weight_load.wait()
    weights[...] = jnp.zeros_like(weights)
    lag_count = weight_ref.shape[0]
    weights[0:ranks, 0:lag_count] = weight_ref[...].T
    weight = weights[band_rows, :]
    far = -(-LAGMAX // LANES)
    ahead = far * LANES - LAGMAX
    errors_width = span + LANES
    past = window[:, 0:third]
    mid = window[:, third : 2 * third]
    future = window[:, 2 * third : 3 * third]
    short, shifts = [], []
    long = jnp.zeros((band, 1), jnp.float32)
    for index in range(lag_count):
        lag = lags_ref[index]
        here = weight[:, index : index + 1]
        is_long = lag >= LANES
        short.append(jnp.where(is_long, 0.0, here))
        long = long + jnp.where(is_long, here, 0.0)
        shifts.append(jnp.where(is_long, 0, lag))
    near = long * pltpu.roll(past, third - ahead, 1)[:, 0:errors_width]
    later = long * pltpu.roll(mid, third - ahead, 1)[:, 0:errors_width]
    for index in range(lag_count):
        near = near + short[index] * pltpu.roll(mid, shifts[index], 1)[:, LANES:]
        later = later + short[index] * pltpu.roll(future, shifts[index], 1)[:, LANES:]
    columns = lax.broadcasted_iota(jnp.int32, (band, errors_width), 1) + tm * span
    errors = jnp.where(
        jnp.logical_and(columns >= LAGMAX, columns < tms * span), mid[:, LANES:] - near, 0.0
    )
    later_columns = columns + (far - 1) * LANES
    later_errors = jnp.where(
        jnp.logical_and(later_columns >= LAGMAX, later_columns < tms * span), future[:, LANES:] - later, 0.0
    )
    carried = long * pltpu.roll(later_errors, errors_width - (LANES - ahead), 1)[:, 0:span]
    for index in range(lag_count):
        carried = carried + short[index] * pltpu.roll(errors, errors_width - shifts[index], 1)[:, 0:span]
    adjoint = errors[:, 0:span] - carried
    regular = LAM_AR * adjoint + LAM_X * time_own

    for j in range(pairs):
        pair_copy(last, j).wait_recv()
        sums[last, j] = parts[last, 2 * j + core] + pair[last, j]
        if pairs > 1:
            @pl.when(j != my_pair)
            def _(j=j):
                sum_copy(last, j, my_pair).start()

    total = sums[last, my_pair]
    for s in range(steps):
        for j in range(pairs):
            if s < last:
                sum_copy(s, j, j).wait_recv()
                total = total + landed[s, j]
            elif pairs > 1:
                @pl.when(j != my_pair)
                def _(j=j):
                    sum_copy(last, j, j).wait_recv()

                total = total + jnp.where(j == my_pair, 0.0, landed[last, j])
    turned = total.T
    gradient = jnp.concatenate([turned[0:ranks], turned[ranks : 2 * ranks]], axis=1)
    own_chunk = factor[last]
    own = own_chunk[:, 0:share]
    for d in range(1, members):
        own = jnp.where(tm % members == d, own_chunk[:, d * share : (d + 1) * share], own)
    gradient = DATA_WEIGHT * gradient + LAM_F * own
    first_load.wait()
    second_load.wait()
    new_first = BETA_ONE * first_ref[...] + (1.0 - BETA_ONE) * gradient
    new_second = BETA_TWO * second_ref[...] + (1.0 - BETA_TWO) * gradient * gradient
    update = (
        LEARNING_RATE * (new_first / BIAS_FIRST) / (jnp.sqrt(new_second / BIAS_SECOND) + ADAM_EPS)
    )
    new_first_ref[...] = new_first
    new_second_ref[...] = new_second
    new_factor_ref[...] = own - update

    data = time_part[band_rows, :]
    for k in range(1, feeders):
        time_copy(k).wait_recv()
        data = data + time_landed[k - 1]
    time_grad_ref[...] = DATA_WEIGHT * data + regular

    for index in range(len(pieces)):
        @pl.when(halo_goes(index))
        def _(index=index):
            halo_copy(index).wait_send()

    for k in range(1, feeders):
        time_copy(k).wait_send()
    for s in range(steps):
        for j in range(pairs):
            pair_copy(s, j).wait_send()
            if s < last:
                sum_copy(s, j, my_pair).wait_send()
            elif pairs > 1:
                @pl.when(j != my_pair)
                def _(s=s, j=j):
                    sum_copy(s, j, my_pair).wait_send()


def hand_over(a, b, c, d, a_out, b_out, c_out, d_out, a_held, b_held, c_held, d_held, sem):
    triples = [(a, a_held, a_out), (b, b_held, b_out), (c, c_held, c_out), (d, d_held, d_out)]
    come = [pltpu.make_async_copy(t[0], t[1], sem.at[0, i]) for i, t in enumerate(triples)]
    go = [pltpu.make_async_copy(t[1], t[2], sem.at[1, i]) for i, t in enumerate(triples)]
    for copy in come:
        copy.start()
    for arrival, copy in zip(come, go):
        arrival.wait()
        copy.start()
    for copy in go:
        copy.wait()


def per_device(
    observed, mask_words, feeder_factor, time_factor, ar_weight, lags, moment_first, moment_second
):
    rows, span = observed.shape
    ranks = time_factor.shape[0]
    tms = lax.axis_size("tm")
    feeders = lax.axis_size("feeder")
    share = rows // tms
    members = 2
    while members * share % LANES:
        members *= 2
    chunk = members * share
    steps = rows // chunk
    pairs = members // 2
    half = share // 2
    band = ranks // feeders
    pieces, slots = halo_pieces(span)
    f32 = jnp.float32
    block = (half, 2 * ranks)
    dma = pltpu.SemaphoreType.DMA
    vmem = pl.BlockSpec(memory_space=pltpu.VMEM)
    hbm = pl.BlockSpec(memory_space=pl.ANY)
    flops = 2 * rows * span * ranks * 4
    results = pl.pallas_call(
        functools.partial(kernel, feeders, tms, chunk, share),
        out_shape=[jax.ShapeDtypeStruct((ranks, share), f32)] * 3
        + [jax.ShapeDtypeStruct((band, span), f32)],
        in_specs=[hbm, hbm, hbm, hbm, hbm, pl.BlockSpec(memory_space=pltpu.SMEM), hbm, hbm],
        out_specs=[vmem] * 4,
        scratch_shapes=[
            pltpu.VMEM((steps, chunk, span), jnp.bfloat16),
            pltpu.VMEM((steps, span // 8, chunk), jnp.int32),
            pltpu.VMEM((steps, ranks, chunk), f32),
            pltpu.VMEM((ranks, span), f32),
            pltpu.VMEM(ar_weight.shape, f32),
            pltpu.VMEM((ranks, share), f32),
            pltpu.VMEM((ranks, share), f32),
            pltpu.VMEM((ranks + span // 8, 2 * span), jnp.bfloat16),
            pltpu.VMEM((2 * span, 2 * ranks), jnp.bfloat16),
            pltpu.VMEM((band, slots * LANES), f32),
            pltpu.VMEM((ranks, LANES), f32),
            pltpu.VMEM((steps, members) + block, f32),
            pltpu.VMEM((steps, pairs) + block, f32),
            pltpu.VMEM((steps, pairs) + block, f32),
            pltpu.VMEM((steps, pairs) + block, f32),
            pltpu.VMEM((ranks, span), f32),
            pltpu.VMEM((feeders - 1, band, span), f32),
            dma((3, steps)),
            dma((4,)),
            dma((steps, pairs)),
            dma((steps, pairs)),
            dma((steps, pairs)),
            dma((steps, pairs)),
            dma((feeders - 1,)),
            dma((feeders - 1,)),
            dma((len(pieces),)),
            dma((len(pieces),)),
        ],
        compiler_params=pltpu.CompilerParams(
            collective_id=0, has_side_effects=True, vmem_limit_bytes=63 * 1024 * 1024
        ),
        cost_estimate=pl.CostEstimate(flops=flops, bytes_accessed=rows * span * 3, transcendentals=0),
    )(
        observed, mask_words.T, feeder_factor.T, time_factor, ar_weight, lags,
        moment_first.T, moment_second.T,
    )
    new_factor, new_first, new_second, time_grad = pl.pallas_call(
        hand_over,
        out_shape=[jax.ShapeDtypeStruct(result.shape, f32) for result in results],
        in_specs=[hbm] * 4,
        out_specs=[hbm] * 4,
        scratch_shapes=[pltpu.VMEM(result.shape, f32) for result in results] + [dma((2, 4))],
    )(*results)
    return (new_factor.T, new_first.T, new_second.T, time_grad)


def solution(mesh):
    placed = (
        P("feeder", "tm"),
        P("feeder", "tm"),
        P("feeder", None),
        P(None, "tm"),
        P(),
        P(),
        P(("feeder", "tm"), None),
        P(("feeder", "tm"), None),
    )
    return jax.shard_map(
        per_device,
        mesh=mesh,
        in_specs=placed,
        out_specs=(
            P(("feeder", "tm"), None),
            P(("feeder", "tm"), None),
            P(("feeder", "tm"), None),
            P("feeder", "tm"),
        ),
        check_vma=False,
    )
```
